512 devices in a mesh: wide: 64 (over y, z), narrow: 8 (over x, core).
Axes of the slice: x: 4, y: 4, z: 16, core: 2. Of those that a mesh axis runs over, the one named last changes fastest.
Arguments:
- images: float32 [2048, 3, 1024], P(('wide', 'narrow')), may hold values from -12 to 12
- block_slot: int32 [1024], replicated, may hold values from 0 to 1023, as said below
- pairs: int32 [512, 64, 2], P(('wide', 'narrow')), may hold values from 0 to 1023, as said below
Outputs:
- row_tiles: float32 [512, 64, 4], P(('wide', 'narrow'))
- col_tiles: float32 [512, 64, 4], P(('wide', 'narrow'))
The draws below stay inside these ranges and needn't reach their ends.
Inputs may be any that keep to these rules, and one draw needn't show every extreme that they name: `block_slot`: a permutation of the block numbers. Storage slot s lies on device s // 2. For device d = w * 8 + n and slot j, block pairs[d, j, 0] is stored on device w * 8 + j // 8 and block pairs[d, j, 1] on device j * 8 + n; every block is the column block of some slot.
All inputs are finite; a program needn't handle non-finite values.
Results may differ from the reference program's by a relative error of at most 0.00002.
Values sent between devices are 32-bit elements; how exact they have to be, the bound alone decides.
No kernel may reach another device: no remote copies, remote signals or barrier semaphores. Data moves between devices by JAX's collectives and lax.ppermute only.
A program may use at most 64 MiB of HBM per device.

```python
import math
import jax
import jax.numpy as jnp
from jax import lax

BLOCK = 2
BLK_DEV = 2
CH = 3
SIDE = 32
LAYERS = 4
POS = 1024
NBLOCKS = 1024
IMAGES = 2048
N_WIDE = 64
N_NARROW = 8


def layout_draw(key):
    slot_of_block = jax.random.permutation(jax.random.fold_in(key, 1), NBLOCKS).astype(jnp.int32)
    block_of_slot = jnp.zeros((NBLOCKS,), jnp.int32).at[slot_of_block].set(jnp.arange(NBLOCKS, dtype=jnp.int32))
    return (slot_of_block, block_of_slot)


def draw_block_slot(key, part):
    shared = layout_draw(key)
    return shared[0]


def draw_pairs(key, part):
    shared = layout_draw(key)
    block_of_slot = shared[1]
    key = jax.random.fold_in(key, 7)
    key_rows, key_shift = jax.random.split(key, 2)
    per_narrow = N_WIDE // N_NARROW
    worker = jnp.arange(N_WIDE * N_NARROW, dtype=jnp.int32)[:, None]
    peer_idx = jnp.arange(N_WIDE, dtype=jnp.int32)[None, :]
    wide_index = worker // N_NARROW
    narrow_index = worker % N_NARROW
    row_device = wide_index * N_NARROW + peer_idx // per_narrow
    col_device = peer_idx * N_NARROW + narrow_index
    row_local = jax.random.randint(key_rows, (N_WIDE * N_NARROW, N_WIDE), 0, BLK_DEV, dtype=jnp.int32)
    shift_of = jax.random.randint(key_shift, (N_WIDE * N_NARROW,), 0, BLK_DEV, dtype=jnp.int32)
    col_local = (wide_index + shift_of[col_device]) % BLK_DEV
    row_block = block_of_slot[row_device * BLK_DEV + row_local]
    col_block = block_of_slot[col_device * BLK_DEV + col_local]
    return jnp.stack([row_block, col_block], axis=-1).astype(jnp.int32)


def draw_images(key, part):
    key = jax.random.fold_in(key, 11)
    key_common, key_noise, key_scale, key_mixing = jax.random.split(key, 4)
    common = jax.random.normal(key_common, (CH, POS), jnp.float32)
    own_noise = jax.random.normal(key_noise, (IMAGES, CH, POS), jnp.float32)
    magnitude = jnp.exp(jax.random.uniform(key_scale, (IMAGES, 1, 1), jnp.float32, math.log(0.5), math.log(2.0)))
    mixing = jax.random.uniform(key_mixing, (IMAGES, 1, 1), jnp.float32, 0.0, 0.9)
    values_out = magnitude * (mixing * common[None] + jnp.sqrt(1.0 - mixing * mixing) * own_noise)
    return jnp.clip(values_out, -12.0, 12.0)


def setup_inputs(seed: int = 0) -> dict:
    streams_of = jax.random.split(jax.random.key(seed), 4)
    images = draw_images(jax.random.fold_in(streams_of[3], 71), 0)
    block_slot = draw_block_slot(jax.random.fold_in(streams_of[3], 71), 0)
    pairs = draw_pairs(jax.random.fold_in(streams_of[3], 71), 0)
    return {"images": images, "block_slot": block_slot, "pairs": pairs}


SIGMA_W = 2.0
SIGMA_B = 0.1
PI_VALUE = math.pi

def shift_flat(values_in, offset):
    pad_shape = values_in.shape[:-1] + (abs(offset),)
    zeros_pad = jnp.zeros(pad_shape, values_in.dtype)
    if offset > 0:
        return jnp.concatenate([values_in[..., offset:], zeros_pad], -1)
    return jnp.concatenate([zeros_pad, values_in[..., :offset]], -1)

def box_mean(values_in):
    column = lax.rem(lax.iota(jnp.int32, values_in.shape[-1]), jnp.int32(SIDE))
    to_right = jnp.where(column < SIDE - 1, shift_flat(values_in, 1), 0.0)
    to_left = jnp.where(column > 0, shift_flat(values_in, -1), 0.0)
    row_sum = values_in + to_right + to_left
    return (row_sum + shift_flat(row_sum, SIDE) + shift_flat(row_sum, -SIDE)) / 9.0

def relu_expect(covariance, var_first, var_second):
    magnitude = jnp.sqrt(var_first * var_second)
    cosine = jnp.clip(covariance / magnitude, -1.0, 1.0)
    angle_rad = jnp.arccos(cosine)
    return magnitude * (jnp.sin(angle_rad) + (PI_VALUE - angle_rad) * cosine) / (2.0 * PI_VALUE)

def variance_maps(block_data):
    variance = SIGMA_W * box_mean(lax.optimization_barrier(jnp.mean(block_data * block_data, axis=-2))) + SIGMA_B
    var_list = [variance]
    for level_idx in range(1, LAYERS):
        variance = SIGMA_W * box_mean(0.5 * variance) + SIGMA_B
        var_list.append(variance)
    return jnp.stack(var_list, axis=-2)

def pair_kernel(row_data, row_vars, col_data, col_vars):
    inner_sum = row_data[..., :, None, 0, :] * col_data[..., None, :, 0, :]
    for channel in range(1, CH):
        inner_sum = inner_sum + row_data[..., :, None, channel, :] * col_data[..., None, :, channel, :]
    covariance = SIGMA_W * box_mean(inner_sum / CH) + SIGMA_B
    for level_idx in range(LAYERS):
        after_relu = relu_expect(covariance, row_vars[..., :, None, level_idx, :], col_vars[..., None, :, level_idx, :])
        if level_idx < LAYERS - 1:
            covariance = SIGMA_W * box_mean(after_relu) + SIGMA_B
    return SIGMA_W * lax.optimization_barrier(jnp.mean(after_relu, axis=-1)) + SIGMA_B

def reference(images, block_slot, pairs):
    blocks = images.reshape(NBLOCKS, BLOCK, CH, POS)
    all_vars = variance_maps(blocks)

    def one_device(device_pairs):
        slot_ids = block_slot[device_pairs]
        return pair_kernel(blocks[slot_ids[:, 0]], all_vars[slot_ids[:, 0]], blocks[slot_ids[:, 1]], all_vars[slot_ids[:, 1]])
    pair_tiles = lax.map(one_device, pairs)
    per_narrow = N_WIDE // N_NARROW
    flat_tiles = pair_tiles.reshape(N_WIDE, N_NARROW, N_NARROW, per_narrow, BLOCK * BLOCK)
    row_tiles = flat_tiles.transpose(0, 2, 1, 3, 4).reshape(N_WIDE * N_NARROW, N_WIDE, BLOCK * BLOCK)
    flipped = jnp.swapaxes(pair_tiles, -1, -2).reshape(N_WIDE, N_NARROW, N_WIDE, BLOCK * BLOCK)
    col_tiles = flipped.transpose(2, 1, 0, 3).reshape(N_WIDE * N_NARROW, N_WIDE, BLOCK * BLOCK)
    return (row_tiles, col_tiles)
```

```python
import math

import jax
import jax.numpy as jnp
from jax import lax
from jax.experimental import pallas as pl
from jax.experimental.pallas import tpu as pltpu
from jax.sharding import PartitionSpec as P

CH = 3
LAYERS = 4
POS = 1024
SIGMA_B = 0.1
BOTH = ("wide", "narrow")

IMG_ROWS = 96
ROWS = 104

X_SCALE = math.sqrt(2.0 / 27.0)
S_SCALE = math.sqrt(1.0 / (9.0 * math.pi))
TILE_SCALE = 9.0 / POS

H_POLY = (
    0.9428086134122584,
    0.04716169007693601,
    0.007401889707478926,
    0.002302233746421043,
    -0.00029199724221271717,
    0.0006175274818372866,
)


def flat(A, L, N):
    return (A * 8 + L) * 8 + N


def to_worker():
    return [
        (flat(a, l, q), flat(q, l ^ (4 * ((a ^ q) & 1)), a))
        for a in range(8)
        for l in range(8)
        for q in range(8)
    ]


def low_groups():
    return [[a * 8 + l for l in range(8)] for a in range(8)]


def return_groups():
    groups = []
    for n in range(8):
        for m in range(n + 1, 8):
            groups.append([flat(n, l, m) for l in range(8)] + [flat(m, l, n) for l in range(8)])
    for n in range(0, 8, 2):
        groups.append([flat(n, l, n) for l in range(8)] + [flat(n + 1, l, n + 1) for l in range(8)])
    return groups


def lane_iota(rows=8):
    return lax.broadcasted_iota(jnp.int32, (rows, 128), 1)


def sub_iota():
    return lax.broadcasted_iota(jnp.int32, (8, 128), 0)


def pack_kernel(images_ref, table_ref, pairs_ref, out_ref):
    wanted = pairs_ref[...]
    low = jnp.broadcast_to(wanted & 127, (8, 128))
    found = jnp.take_along_axis(table_ref[...], low, axis=1)
    mine = jnp.where(sub_iota() == jnp.broadcast_to(wanted >> 7, (8, 128)), found & 1, 0)
    local = jnp.sum(mine.astype(jnp.float32), axis=0, keepdims=True)
    for image in range(4):
        for channel in range(CH):
            for part in range(8):
                row = image * 24 + channel * 8 + part
                out_ref[0, row : row + 1, :] = (
                    images_ref[image, channel : channel + 1, part * 128 : (part + 1) * 128] * X_SCALE
                )
    out_ref[0, IMG_ROWS:ROWS, :] = jnp.broadcast_to(local, (8, 128))
    for peer in range(1, 8):
        out_ref[peer] = out_ref[0]


def relay_kernel(own_ref, near_ref, out_ref):
    out_ref[:IMG_ROWS, :] = own_ref[0, :IMG_ROWS, :]
    for n in range(8):
        out_ref[IMG_ROWS + n : IMG_ROWS + n + 1, :] = near_ref[n, 0:1, :]


def box_sum(x, masks):
    first_row, last_row, first_col, last_col = masks
    above = jnp.where(first_row, 0.0, pltpu.roll(x[3], 1, 0))
    below = jnp.where(last_row, 0.0, pltpu.roll(x[0], 7, 0))
    top, bottom = x[0] + x[1], x[2] + x[3]
    sums = [top + above, top + x[2], bottom + x[1], bottom + below]
    return [
        t + jnp.where(first_col, 0.0, pltpu.roll(t, 1, 1)) + jnp.where(last_col, 0.0, pltpu.roll(t, 127, 1))
        for t in sums
    ]


def tile_kernel(col_ref, row_ref, rows_out, cols_out, xr, xc, rr, rc, sr, sc, ta, tb, info, sem):
    high, near = lax.axis_index("wide") // 8, lax.axis_index("narrow")
    place = lax.axis_index("wide") % 8
    turn = ((high ^ near) & 1) * 4
    base = high * 16 + place * 2
    copy = pltpu.make_async_copy(row_ref.at[:, pl.ds(IMG_ROWS, 8), :], info, sem)
    copy.start()

    lane, sub = lane_iota(), sub_iota()
    column = lane & 31
    masks = (sub == 0, sub == 7, column == 0, column == 31)

    def prepare(source, block, x_out, r_out, s_out, first_image):
        device, local = block // 2, block % 2
        square = [None] * 4
        for channel in range(CH):
            start = pl.multiple_of(local * 48 + channel * 8, 8)
            one = source[device, pl.ds(start, 8), :]
            two = source[device, pl.ds(pl.multiple_of(start + 24, 8), 8), :]
            for v in range(4):
                index = column + 32 * v
                x = jnp.where(
                    first_image,
                    jnp.take_along_axis(one, index, axis=1),
                    jnp.take_along_axis(two, index, axis=1),
                )
                x_out[block, channel * 4 + v] = x
                square[v] = x * x if channel == 0 else square[v] + x * x
        variance = [b + SIGMA_B for b in box_sum(square, masks)]
        for level in range(LAYERS):
            for v in range(4):
                root = jnp.sqrt(variance[v])
                r_out[block, level * 4 + v] = 1.0 / root
                s_out[block, level * 4 + v] = root * S_SCALE
            if level < LAYERS - 1:
                variance = [b * (1.0 / 9.0) + SIGMA_B for b in box_sum(variance, masks)]

    def prepare_both(block, carry):
        prepare(row_ref, block, xr, rr, sr, lane < 64)
        prepare(col_ref, block, xc, rc, sc, (lane & 32) == 0)
        return carry

    lax.fori_loop(0, 16, prepare_both, 0)
    copy.wait()

    def one_pair(l, n):
        place_l = l ^ turn
        rb = place_l * 2 + info[place_l, n, base].astype(jnp.int32)
        cb = n * 2 + info[place_l, n, base + 1].astype(jnp.int32)
        products = []
        for v in range(4):
            t = xr[rb, v] * xc[cb, v]
            for channel in range(1, CH):
                t = t + xr[rb, channel * 4 + v] * xc[cb, channel * 4 + v]
            products.append(t)
        covariance = [b + SIGMA_B for b in box_sum(products, masks)]
        for level in range(LAYERS):
            relu = []
            for v in range(4):
                at = level * 4 + v
                cosine = covariance[v] * (rr[rb, at] * rc[cb, at])
                w = jnp.maximum(1.0 - jnp.abs(cosine), 1e-30)
                poly = H_POLY[-1] * w + H_POLY[-2]
                for coefficient in H_POLY[-3::-1]:
                    poly = poly * w + coefficient
                h = (w * w) * lax.rsqrt(w) * poly + math.pi * jnp.minimum(jnp.maximum(cosine, 0.0), 1.0)
                relu.append(h * (sr[rb, at] * sc[cb, at]))
            if level < LAYERS - 1:
                covariance = [b + SIGMA_B for b in box_sum(relu, masks)]
        total = jnp.sum((relu[0] + relu[1]) + (relu[2] + relu[3]), axis=0, keepdims=True)
        ta[pl.ds(n * 8 + l, 1), :] = total
        tb[pl.ds(l * 8 + n, 1), :] = total

    def some_pairs(step, carry):
        for u in range(4):
            one_pair(step // 2, (step % 2) * 4 + u)
        return carry

    lax.fori_loop(0, 16, some_pairs, 0)

    def gathered(ref, index):
        out = jnp.zeros((8, 128), jnp.float32)
        for g in range(8):
            t = ref[g * 8 : g * 8 + 8, :]
            for shift in (1, 2, 4, 8, 16):
                t = t + pltpu.roll(t, 128 - shift, 1)
            out = jnp.where(lane >> 2 == g, jnp.take_along_axis(t, index, axis=1), out)
        return out * TILE_SCALE + SIGMA_B

    rows = gathered(ta, (lane & 3) * 32)
    rows_out[0:8, :] = rows
    rows_out[8:16, :] = rows
    cols_out[...] = gathered(tb, (lane & 1) * 64 + ((lane >> 1) & 1) * 32)


def place_kernel(rows_ref, cols_ref, rows_out, cols_out):
    high, near = lax.axis_index("wide") // 8, lax.axis_index("narrow")
    half = jnp.where(high == near, high & 1, jnp.where(high < near, 1, 0))
    rows = rows_ref[pl.ds(pl.multiple_of(half * 8, 8), 8), :]
    cols = cols_ref[...]
    for g in range(8):
        shift = (128 - 4 * g) % 128
        rows_out[0, g * 8 : g * 8 + 8, :] = (pltpu.roll(rows, shift, 1) if shift else rows)[:, :4]
        cols_out[0, pl.ds(g, 8, stride=8), :] = (pltpu.roll(cols, shift, 1) if shift else cols)[:, :4]


def f32(*shape):
    return jax.ShapeDtypeStruct(shape, jnp.float32)


def whole(count):
    return [pl.BlockSpec(memory_space=pltpu.VMEM)] * count


def params():
    return pltpu.CompilerParams(vmem_limit_bytes=32 * 1024 * 1024)


def shards(images, block_slot, pairs):
    packed = pl.pallas_call(
        pack_kernel,
        out_shape=f32(8, ROWS, 128),
        in_specs=whole(3),
        out_specs=pl.BlockSpec(memory_space=pltpu.VMEM),
        compiler_params=params(),
    )(images, block_slot.reshape(8, 128), pairs.reshape(1, 128))
    near = lax.all_to_all(packed, "narrow", split_axis=0, concat_axis=0, tiled=True)
    relayed = pl.pallas_call(
        relay_kernel,
        out_shape=f32(ROWS, 128),
        grid=(1,),
        in_specs=[
            pl.BlockSpec((1, ROWS, 128), lambda i: (0, 0, 0)),
            pl.BlockSpec((8, 8, 128), lambda i: (0, IMG_ROWS // 8, 0)),
        ],
        out_specs=pl.BlockSpec((ROWS, 128), lambda i: (0, 0)),
        compiler_params=params(),
    )(packed, near)
    moved = lax.ppermute(relayed, BOTH, to_worker())
    far = lax.all_to_all(
        jnp.broadcast_to(moved[None], (8, ROWS, 128)),
        "wide",
        split_axis=0,
        concat_axis=0,
        tiled=True,
        axis_index_groups=low_groups(),
    )
    row_send, col_send = pl.pallas_call(
        tile_kernel,
        out_shape=(f32(16, 128), f32(8, 128)),
        in_specs=whole(2),
        out_specs=tuple(whole(2)),
        scratch_shapes=[
            pltpu.VMEM((16, 4 * CH, 8, 128), jnp.float32),
            pltpu.VMEM((16, 4 * CH, 8, 128), jnp.float32),
            pltpu.VMEM((16, 4 * LAYERS, 8, 128), jnp.float32),
            pltpu.VMEM((16, 4 * LAYERS, 8, 128), jnp.float32),
            pltpu.VMEM((16, 4 * LAYERS, 8, 128), jnp.float32),
            pltpu.VMEM((16, 4 * LAYERS, 8, 128), jnp.float32),
            pltpu.VMEM((64, 128), jnp.float32),
            pltpu.VMEM((64, 128), jnp.float32),
            pltpu.SMEM((8, 8, 128), jnp.float32),
            pltpu.SemaphoreType.DMA,
        ],
        compiler_params=params(),
    )(near, far)
    row_got = lax.all_to_all(
        row_send, BOTH, split_axis=0, concat_axis=0, tiled=True, axis_index_groups=return_groups()
    )
    col_got = lax.all_to_all(col_send, "narrow", split_axis=0, concat_axis=0, tiled=True)
    return pl.pallas_call(
        place_kernel,
        out_shape=(f32(1, 64, 4), f32(1, 64, 4)),
        in_specs=whole(2),
        out_specs=tuple(whole(2)),
        compiler_params=params(),
    )(row_got, col_got)


def solution(mesh):
    spec = P(BOTH, None, None)
    return jax.shard_map(
        shards, mesh=mesh, in_specs=(spec, P(), spec), out_specs=(spec, spec), check_vma=False
    )
```

```python
import math

import jax
import jax.numpy as jnp
from jax import lax
from jax.experimental import pallas as pl
from jax.experimental.pallas import tpu as pltpu
from jax.sharding import PartitionSpec as P

CH = 3
LAYERS = 4
POS = 1024
SIGMA_B = 0.1
BOTH = ("wide", "narrow")

IMG_ROWS = 96
ROWS = 104

X_SCALE = math.sqrt(2.0 / 27.0)
H_SCALE = 1.0 / (9.0 * math.pi)
H_LINE = math.pi * H_SCALE
TILE_SCALE = 9.0 / POS

H_POLY = tuple(
    H_SCALE * value
    for value in (
    0.9428086134122584,
    0.04716169007693601,
    0.007401889707478926,
    0.002302233746421043,
    -0.00029199724221271717,
    0.0006175274818372866,
    )
)


def flat(A, L, N):
    return (A * 8 + L) * 8 + N


def worker_narrow(a, q):
    return (2 * (q // 2) + 2 - a // 2) % 4 * 2 + a % 2


def worker_low(l, turn, slot):
    if not turn:
        return l ^ (4 * slot)
    if (l & 1) == slot:
        return ((l >> 1) + 3) & 3
    return 4 + (((l >> 1) + 1) & 3)


def row_routes(slot):
    return [
        (flat(a, l, q), flat(q, worker_low(l, (a ^ q) & 1, slot), worker_narrow(a, q)))
        for a in range(8)
        for l in range(8)
        for q in range(8)
    ]


def low_groups():
    return [[g * 4 + l for l in range(4)] for g in range(16)]


def lane_iota(rows=8):
    return lax.broadcasted_iota(jnp.int32, (rows, 128), 1)


def sub_iota():
    return lax.broadcasted_iota(jnp.int32, (8, 128), 0)


def pack_kernel(images_ref, table_ref, pairs_ref, out_ref, rows, wide):
    lane = lane_iota()
    wide[...] = jnp.zeros((8, 128), jnp.int32)
    wide[0:2, 0:64] = pairs_ref[...]
    slots = wide[...]
    wanted = jnp.where(lane < 64, slots[0:1, :], pltpu.roll(slots, 64, 1)[1:2, :])
    found = jnp.take_along_axis(table_ref[...], wanted & 127, axis=1)
    mine = jnp.where(sub_iota() == wanted >> 7, found & 1, 0)
    out_ref[0, IMG_ROWS:, :] = jnp.broadcast_to(jnp.sum(mine.astype(jnp.float32), axis=0, keepdims=True), (8, 128))
    for channel in range(CH):
        for part in range(8):
            values = images_ref[channel, :, part * 128 : (part + 1) * 128] * X_SCALE
            for image in range(4):
                rows[image * CH + channel, part : part + 1, :] = values[image : image + 1, :]
    index = (lane & 64) // 2 + (lane & 31)
    for block in range(2):
        for channel in range(CH):
            for u in range(2):
                one, two = (
                    jnp.take_along_axis(rows[(block * 2 + i) * CH + channel], index + 64 * u, axis=1)
                    for i in range(2)
                )
                start = ((block * CH + channel) * 2 + u) * 8
                out_ref[0, start : start + 8, :] = jnp.where((lane & 32) == 0, one, two)
    for peer in range(1, 8):
        out_ref[peer] = out_ref[0]


def relay_kernel(own_ref, near_ref, out_ref):
    out_ref[:IMG_ROWS, :] = own_ref[0, :IMG_ROWS, :]
    for n in range(8):
        out_ref[IMG_ROWS + n : IMG_ROWS + n + 1, :] = near_ref[n, IMG_ROWS : IMG_ROWS + 1, :]


def spread_kernel(first_ref, second_ref, out_ref):
    for peer in range(4):
        out_ref[peer, 0] = first_ref[...]
        out_ref[peer, 1] = second_ref[...]


def box_sum(x, masks):
    first_row, last_row, first_col, last_col = masks
    above = jnp.where(first_row, 0.0, pltpu.roll(x[3], 1, 0))
    below = jnp.where(last_row, 0.0, pltpu.roll(x[0], 7, 0))
    top, bottom = x[0] + x[1], x[2] + x[3]
    sums = [top + above, top + x[2], bottom + x[1], bottom + below]
    return [
        t + jnp.where(first_col, 0.0, pltpu.roll(t, 1, 1)) + jnp.where(last_col, 0.0, pltpu.roll(t, 127, 1))
        for t in sums
    ]


def constants():
    lane, sub = lane_iota(), sub_iota()
    column = lane & 31
    masks = (sub == 0, sub == 7, column == 0, column == 31)
    return lane, masks, (lane & 64) // 2 + column, (lane & 32) + column


def prepare(read, block, local, x_out, v_out, index, masks):
    square = [None] * 4
    for channel in range(CH):
        for v in range(4):
            tile = read(local * 48 + channel * 16 + (v // 2) * 8)
            x = jnp.take_along_axis(tile, index + 64 * (v % 2), axis=1)
            x_out[block, channel * 4 + v] = x
            square[v] = x * x if channel == 0 else square[v] + x * x
    for v, b in enumerate(box_sum(square, masks)):
        v_out[block, v] = b + SIGMA_B


def deepen(block, v_out, level, masks):
    variance = [v_out[block, (level - 1) * 4 + v] for v in range(4)]
    for v, b in enumerate(box_sum(variance, masks)):
        v_out[block, level * 4 + v] = b * (1.0 / 9.0) + SIGMA_B


def pair_sums(blocks, xr, xc, vr, vc, masks):
    found = []
    for rb, cb in blocks:
        products = []
        for v in range(4):
            t = xr[rb, v] * xc[cb, v]
            for channel in range(1, CH):
                t = t + xr[rb, channel * 4 + v] * xc[cb, channel * 4 + v]
            products.append(t)
        found.append((rb, cb, products))
    for level in range(LAYERS):
        nexts = []
        for rb, cb, products in found:
            covariance = [b + SIGMA_B for b in box_sum(products, masks)]
            relu = []
            for v in range(4):
                at = level * 4 + v
                square = vr[rb, at] * vc[cb, at]
                inverse = lax.rsqrt(square)
                cosine = covariance[v] * inverse
                w = jnp.maximum(1.0 - jnp.abs(cosine), 1e-30)
                poly = H_POLY[-1] * w + H_POLY[-2]
                for coefficient in H_POLY[-3::-1]:
                    poly = poly * w + coefficient
                h = (w * w) * lax.rsqrt(w) * poly + H_LINE * jnp.minimum(jnp.maximum(cosine, 0.0), 1.0)
                relu.append(h * (square * inverse))
            nexts.append((rb, cb, relu))
        found = nexts
    return [
        jnp.sum((relu[0] + relu[1]) + (relu[2] + relu[3]), axis=0, keepdims=True) for rb, cb, relu in found
    ]


def col_kernel(near_ref, xc, vc):
    lane, masks, by_row, by_col = constants()

    def some(step, carry):
        for u in range(8):
            device = step * 4 + u // 2
            read = lambda start: near_ref[device, start : start + 8, :]
            prepare(read, step * 8 + u, u % 2, xc, vc, by_col, masks)
        return carry

    lax.fori_loop(0, 2, some, 0)
    for level in range(1, LAYERS):

        def deeper(step, carry):
            for u in range(8):
                deepen(step * 8 + u, vc, level, masks)
            return carry

        lax.fori_loop(0, 2, deeper, 0)


def choice_lane():
    return lax.axis_index("wide")


def own_kernel(first_ref, second_ref, xc, vc, sums_out, xr, vr, info, sems):
    base = choice_lane()
    copies = []
    for slot, ref in enumerate((first_ref, second_ref)):
        copies.append(pltpu.make_async_copy(ref.at[pl.ds(IMG_ROWS, 8), :], info.at[slot], sems.at[slot]))
        copies[-1].start()
    lane, masks, by_row, by_col = constants()
    for slot, ref in enumerate((first_ref, second_ref)):
        for local in range(2):
            prepare(lambda start: ref[start : start + 8, :], slot * 2 + local, local, xr, vr, by_row, masks)
    for level in range(1, LAYERS):
        for block in range(4):
            deepen(block, vr, level, masks)
    for copy in copies:
        copy.wait()

    def some_pairs(slot, carry):
        blocks = []
        for n in range(8):
            rb = slot * 2 + info[slot, n, base].astype(jnp.int32)
            blocks.append((rb, n * 2 + info[slot, n, base + 64].astype(jnp.int32)))
        for n, total in enumerate(pair_sums(blocks, xr, xc, vr, vc, masks)):
            sums_out[pl.ds(slot * 8 + n, 1), :] = total
        return carry

    lax.fori_loop(0, 2, some_pairs, 0)


def tile_kernel(far_ref, own_ref, xc, vc, tiles_out, xr, vr, sums, info, sem):
    high, near = lax.axis_index("wide") // 8, lax.axis_index("narrow")
    place = lax.axis_index("wide") % 8
    turn = ((high ^ near) & 1) == 1
    half, mine = place >> 2, place & 3
    base = choice_lane()
    copy = pltpu.make_async_copy(far_ref.at[:, :, pl.ds(IMG_ROWS, 8), :], info, sem)
    copy.start()
    lane, masks, by_row, by_col = constants()

    def row_at(p, slot):
        side = slot ^ half
        return jnp.where(turn, ((p + 1 + 2 * half) & 3) * 2 + side, p + 4 * side)

    for step in range(3):
        p = (mine + step + 1) & 3
        for slot in range(2):
            for local in range(2):
                read = lambda start: far_ref[p, slot, start : start + 8, :]
                prepare(read, step * 4 + slot * 2 + local, local, xr, vr, by_row, masks)
    for level in range(1, LAYERS):
        for block in range(12):
            deepen(block, vr, level, masks)
    for slot in range(2):
        l = row_at(mine, slot)
        for n in range(8):
            sums[n, pl.ds(l, 1), :] = own_ref[slot * 8 + n : slot * 8 + n + 1, :]
    copy.wait()

    def some_pairs(step, carry):
        p, slot = (mine + step // 2 + 1) & 3, step % 2
        l = row_at(p, slot)
        blocks = []
        for n in range(8):
            rb = step * 2 + info[p, slot, n, base].astype(jnp.int32)
            blocks.append((rb, n * 2 + info[p, slot, n, base + 64].astype(jnp.int32)))
        for n, total in enumerate(pair_sums(blocks, xr, xc, vr, vc, masks)):
            sums[n, pl.ds(l, 1), :] = total
        return carry

    lax.fori_loop(0, 6, some_pairs, 0)

    tiles = []
    rows = jnp.zeros((8, 128), jnp.float32)
    for n in range(8):
        t = sums[n]
        for shift in (1, 2, 4, 8, 16):
            t = t + pltpu.roll(t, 128 - shift, 1)
        t = t * TILE_SCALE + SIGMA_B
        rows = jnp.where(lane >> 2 == n, jnp.take_along_axis(t, (lane & 3) * 32, axis=1), rows)
        tiles.append(jnp.take_along_axis(t, (lane & 1) * 64 + (lane & 2) * 16, axis=1))
    for n in range(8):
        tiles_out[n] = jnp.where(lane < 32, rows, tiles[n])


def order_kernel(tiles_ref, out_ref):
    high = lax.axis_index("wide") // 8
    for a in range(8):
        out_ref[a * 8 : a * 8 + 8, :] = tiles_ref[worker_narrow(a, high)]


def place_kernel(cols_ref, rows_ref, rows_out, cols_out, square):
    near = lax.axis_index("narrow")
    square[0:64, :] = cols_ref[...]
    square[64:72, :] = rows_ref[pl.ds(pl.multiple_of(near * 8, 8), 8), :]
    square[72:128, :] = jnp.zeros((56, 128), jnp.float32)
    turned = square[...].T
    cols_out[...] = turned[32:36, :64]
    lane = lane_iota()
    upper = jnp.where(sub_iota() >= 4, 1, 0)
    rows = jnp.zeros((8, 128), jnp.float32)
    for g in range(4):
        part = jnp.take_along_axis(turned[8 * g : 8 * g + 8, :], 64 + (lane & 7), axis=1)
        rows = jnp.where((lane >> 3) == 2 * g + upper, part, rows)
    rows_out[...] = (rows + pltpu.roll(rows, 4, 0))[:4, :64]


def f32(*shape):
    return jax.ShapeDtypeStruct(shape, jnp.float32)


def whole(count):
    return [pl.BlockSpec(memory_space=pltpu.VMEM)] * count


def params():
    return pltpu.CompilerParams(vmem_limit_bytes=32 * 1024 * 1024)


def call(kernel, outs, *args, scratch=()):
    return pl.pallas_call(
        kernel,
        out_shape=outs,
        in_specs=whole(len(args)),
        out_specs=tuple(whole(len(outs))) if isinstance(outs, tuple) else whole(1)[0],
        scratch_shapes=scratch,
        compiler_params=params(),
    )(*args)


def exchange(x, axis, groups=None):
    return lax.all_to_all(x, axis, split_axis=0, concat_axis=0, tiled=True, axis_index_groups=groups)


def shards(images, block_slot, pairs):
    vmem = lambda *shape: pltpu.VMEM(shape, jnp.float32)
    packed = call(
        pack_kernel,
        f32(8, ROWS, 128),
        images.transpose(1, 0, 2),
        block_slot.reshape(8, 128),
        pairs[0].T,
        scratch=[vmem(4 * CH, 8, 128), pltpu.VMEM((8, 128), jnp.int32)],
    )
    near = exchange(packed, "narrow")
    relayed = call(relay_kernel, f32(ROWS, 128), packed, near)
    first = lax.ppermute(relayed, BOTH, row_routes(0))
    second = lax.ppermute(relayed, BOTH, row_routes(1))
    xc, vc = call(col_kernel, (f32(16, 4 * CH, 8, 128), f32(16, 4 * LAYERS, 8, 128)), near)
    spread = call(spread_kernel, f32(4, 2, ROWS, 128), first, second)
    far = exchange(spread, "wide", low_groups())
    own = call(
        own_kernel,
        f32(16, 128),
        first,
        second,
        xc,
        vc,
        scratch=[
            vmem(4, 4 * CH, 8, 128),
            vmem(4, 4 * LAYERS, 8, 128),
            pltpu.SMEM((2, 8, 128), jnp.float32),
            pltpu.SemaphoreType.DMA((2,)),
        ],
    )
    tiles = call(
        tile_kernel,
        f32(8, 8, 128),
        far,
        own,
        xc,
        vc,
        scratch=[
            vmem(12, 4 * CH, 8, 128),
            vmem(12, 4 * LAYERS, 8, 128),
            vmem(8, 8, 128),
            pltpu.SMEM((4, 2, 8, 128), jnp.float32),
            pltpu.SemaphoreType.DMA,
        ],
    )
    ordered = call(order_kernel, f32(64, 128), exchange(tiles, "narrow"))
    rows, cols = call(
        place_kernel, (f32(4, 64), f32(4, 64)), ordered, exchange(ordered, "wide"), scratch=[vmem(128, 128)]
    )
    return rows.T[None], cols.T[None]


def solution(mesh):
    spec = P(BOTH, None, None)
    return jax.shard_map(
        shards, mesh=mesh, in_specs=(spec, P(), spec), out_specs=(spec, spec), check_vma=False
    )
```

```python
import math

import jax
import jax.numpy as jnp
from jax import lax
from jax.experimental import pallas as pl
from jax.experimental.pallas import tpu as pltpu
from jax.sharding import PartitionSpec as P

CH = 3
LAYERS = 4
POS = 1024
SIGMA_B = 0.1
BOTH = ("wide", "narrow")

IMG_ROWS = 96
ROWS = 104

X_SCALE = math.sqrt(2.0 / 27.0)
H_SCALE = 1.0 / (9.0 * math.pi)
H_LINE = math.pi * H_SCALE
TILE_SCALE = 9.0 / POS

H_POLY = tuple(
    H_SCALE * value
    for value in (
    0.9428086134122584,
    0.04716169007693601,
    0.007401889707478926,
    0.002302233746421043,
    -0.00029199724221271717,
    0.0006175274818372866,
    )
)


def flat(A, L, N):
    return (A * 8 + L) * 8 + N


def worker_narrow(a, q):
    return (2 * (q // 2) + 2 - a // 2) % 4 * 2 + a % 2


def worker_low(l, turn, slot):
    if not turn:
        return l ^ (4 * slot)
    if (l & 1) == slot:
        return ((l >> 1) + 3) & 3
    return 4 + (((l >> 1) + 1) & 3)


def row_routes(slot):
    return [
        (flat(a, l, q), flat(q, worker_low(l, (a ^ q) & 1, slot), worker_narrow(a, q)))
        for a in range(8)
        for l in range(8)
        for q in range(8)
    ]


def home_groups():
    order = [sorted(range(8), key=lambda a: worker_narrow(a, q)) for q in range(8)]
    return [[flat(a, l, q) for a in order[q] for l in range(8)] for q in range(8)]


def low_groups():
    return [[g * 4 + l for l in range(4)] for g in range(16)]


def lane_iota(rows=8):
    return lax.broadcasted_iota(jnp.int32, (rows, 128), 1)


def sub_iota():
    return lax.broadcasted_iota(jnp.int32, (8, 128), 0)


def pack_kernel(images_ref, table_ref, pairs_ref, out_ref, rows, wide):
    lane = lane_iota()
    wide[...] = jnp.zeros((8, 128), jnp.int32)
    wide[0:2, 0:64] = pairs_ref[...]
    slots = wide[...]
    wanted = jnp.where(lane < 64, slots[0:1, :], pltpu.roll(slots, 64, 1)[1:2, :])
    found = jnp.take_along_axis(table_ref[...], wanted & 127, axis=1)
    mine = jnp.where(sub_iota() == wanted >> 7, found & 1, 0)
    out_ref[0, IMG_ROWS:, :] = jnp.broadcast_to(jnp.sum(mine.astype(jnp.float32), axis=0, keepdims=True), (8, 128))
    for channel in range(CH):
        for part in range(8):
            values = images_ref[channel, :, part * 128 : (part + 1) * 128] * X_SCALE
            for image in range(4):
                rows[image * CH + channel, part : part + 1, :] = values[image : image + 1, :]
    index = (lane & 64) // 2 + (lane & 31)
    for block in range(2):
        for channel in range(CH):
            for u in range(2):
                one, two = (
                    jnp.take_along_axis(rows[(block * 2 + i) * CH + channel], index + 64 * u, axis=1)
                    for i in range(2)
                )
                start = ((block * CH + channel) * 2 + u) * 8
                out_ref[0, start : start + 8, :] = jnp.where((lane & 32) == 0, one, two)
    for peer in range(1, 8):
        out_ref[peer] = out_ref[0]


def relay_kernel(own_ref, near_ref, out_ref):
    out_ref[:IMG_ROWS, :] = own_ref[0, :IMG_ROWS, :]
    for n in range(8):
        out_ref[IMG_ROWS + n : IMG_ROWS + n + 1, :] = near_ref[n, IMG_ROWS : IMG_ROWS + 1, :]


def spread_kernel(first_ref, second_ref, out_ref):
    for peer in range(4):
        out_ref[peer, 0] = first_ref[...]
        out_ref[peer, 1] = second_ref[...]


def box_sum(x, masks):
    first_row, last_row, first_col, last_col = masks
    above = jnp.where(first_row, 0.0, pltpu.roll(x[3], 1, 0))
    below = jnp.where(last_row, 0.0, pltpu.roll(x[0], 7, 0))
    top, bottom = x[0] + x[1], x[2] + x[3]
    sums = [top + above, top + x[2], bottom + x[1], bottom + below]
    return [
        t + jnp.where(first_col, 0.0, pltpu.roll(t, 1, 1)) + jnp.where(last_col, 0.0, pltpu.roll(t, 127, 1))
        for t in sums
    ]


def constants():
    lane, sub = lane_iota(), sub_iota()
    column = lane & 31
    masks = (sub == 0, sub == 7, column == 0, column == 31)
    return lane, masks, (lane & 64) // 2 + column, (lane & 32) + column


def prepare(read, block, local, x_out, v_out, index, masks):
    square = [None] * 4
    for channel in range(CH):
        for v in range(4):
            tile = read(local * 48 + channel * 16 + (v // 2) * 8)
            x = jnp.take_along_axis(tile, index + 64 * (v % 2), axis=1)
            x_out[block, channel * 4 + v] = x
            square[v] = x * x if channel == 0 else square[v] + x * x
    for v, b in enumerate(box_sum(square, masks)):
        v_out[block, v] = b + SIGMA_B


def deepen(block, v_out, level, masks):
    variance = [v_out[block, (level - 1) * 4 + v] for v in range(4)]
    for v, b in enumerate(box_sum(variance, masks)):
        v_out[block, level * 4 + v] = b * (1.0 / 9.0) + SIGMA_B


def pair_sums(blocks, xr, xc, vr, vc, masks):
    found = []
    for rb, cb in blocks:
        products = []
        for v in range(4):
            t = xr[rb, v] * xc[cb, v]
            for channel in range(1, CH):
                t = t + xr[rb, channel * 4 + v] * xc[cb, channel * 4 + v]
            products.append(t)
        found.append((rb, cb, products))
    for level in range(LAYERS):
        nexts = []
        for rb, cb, products in found:
            covariance = [b + SIGMA_B for b in box_sum(products, masks)]
            relu = []
            for v in range(4):
                at = level * 4 + v
                square = vr[rb, at] * vc[cb, at]
                inverse = lax.rsqrt(square)
                cosine = covariance[v] * inverse
                w = jnp.maximum(1.0 - jnp.abs(cosine), 1e-30)
                poly = H_POLY[-1] * w + H_POLY[-2]
                for coefficient in H_POLY[-3::-1]:
                    poly = poly * w + coefficient
                h = (w * w) * lax.rsqrt(w) * poly + H_LINE * jnp.minimum(jnp.maximum(cosine, 0.0), 1.0)
                relu.append(h * (square * inverse))
            nexts.append((rb, cb, relu))
        found = nexts
    return [
        jnp.sum((relu[0] + relu[1]) + (relu[2] + relu[3]), axis=0, keepdims=True) for rb, cb, relu in found
    ]


def col_kernel(near_ref, xc, vc):
    lane, masks, by_row, by_col = constants()

    def some(step, carry):
        for u in range(8):
            device = step * 4 + u // 2
            read = lambda start: near_ref[device, start : start + 8, :]
            prepare(read, step * 8 + u, u % 2, xc, vc, by_col, masks)
        return carry

    lax.fori_loop(0, 2, some, 0)
    for level in range(1, LAYERS):

        def deeper(step, carry):
            for u in range(8):
                deepen(step * 8 + u, vc, level, masks)
            return carry

        lax.fori_loop(0, 2, deeper, 0)


def choice_lane():
    return lax.axis_index("wide")


def own_kernel(first_ref, second_ref, xc, vc, sums_out, xr, vr, info, sems):
    base = choice_lane()
    copies = []
    for slot, ref in enumerate((first_ref, second_ref)):
        copies.append(pltpu.make_async_copy(ref.at[pl.ds(IMG_ROWS, 8), :], info.at[slot], sems.at[slot]))
        copies[-1].start()
    lane, masks, by_row, by_col = constants()
    for slot, ref in enumerate((first_ref, second_ref)):
        for local in range(2):
            prepare(lambda start: ref[start : start + 8, :], slot * 2 + local, local, xr, vr, by_row, masks)
    for level in range(1, LAYERS):
        for block in range(4):
            deepen(block, vr, level, masks)
    for copy in copies:
        copy.wait()

    def some_pairs(slot, carry):
        blocks = []
        for n in range(8):
            rb = slot * 2 + info[slot, n, base].astype(jnp.int32)
            blocks.append((rb, n * 2 + info[slot, n, base + 64].astype(jnp.int32)))
        for n, total in enumerate(pair_sums(blocks, xr, xc, vr, vc, masks)):
            sums_out[pl.ds(slot * 8 + n, 1), :] = total
        return carry

    lax.fori_loop(0, 2, some_pairs, 0)


def tile_kernel(far_ref, own_ref, xc, vc, tiles_out, xr, vr, sums, info, sem):
    high, near = lax.axis_index("wide") // 8, lax.axis_index("narrow")
    place = lax.axis_index("wide") % 8
    turn = ((high ^ near) & 1) == 1
    half, mine = place >> 2, place & 3
    base = choice_lane()
    copy = pltpu.make_async_copy(far_ref.at[:, :, pl.ds(IMG_ROWS, 8), :], info, sem)
    copy.start()
    lane, masks, by_row, by_col = constants()

    def row_at(p, slot):
        side = slot ^ half
        return jnp.where(turn, ((p + 1 + 2 * half) & 3) * 2 + side, p + 4 * side)

    for step in range(3):
        p = (mine + step + 1) & 3
        for slot in range(2):
            for local in range(2):
                read = lambda start: far_ref[p, slot, start : start + 8, :]
                prepare(read, step * 4 + slot * 2 + local, local, xr, vr, by_row, masks)
    for level in range(1, LAYERS):
        for block in range(12):
            deepen(block, vr, level, masks)
    for slot in range(2):
        l = row_at(mine, slot)
        for n in range(8):
            sums[n, pl.ds(l, 1), :] = own_ref[slot * 8 + n : slot * 8 + n + 1, :]
    copy.wait()

    def some_pairs(step, carry):
        p = (mine + step + 1) & 3
        for slot in range(2):
            l = row_at(p, slot)
            blocks = []
            for n in range(8):
                rb = step * 4 + slot * 2 + info[p, slot, n, base].astype(jnp.int32)
                blocks.append((rb, n * 2 + info[p, slot, n, base + 64].astype(jnp.int32)))
            for n, total in enumerate(pair_sums(blocks, xr, xc, vr, vc, masks)):
                sums[n, pl.ds(l, 1), :] = total
        return carry

    lax.fori_loop(0, 3, some_pairs, 0)

    tiles = []
    rows = jnp.zeros((8, 128), jnp.float32)
    for n in range(8):
        t = sums[n]
        for shift in (1, 2, 4, 8, 16):
            t = t + pltpu.roll(t, 128 - shift, 1)
        t = t * TILE_SCALE + SIGMA_B
        rows = jnp.where(lane >> 2 == n, jnp.take_along_axis(t, (lane & 3) * 32, axis=1), rows)
        tiles.append(jnp.take_along_axis(t, (lane & 1) * 64 + (lane & 2) * 16, axis=1))
    for n in range(8):
        tiles_out[n] = jnp.where(lane < 32, rows, tiles[n])


def place_kernel(tiles_ref, rows_ref, rows_out, cols_out, square):
    high, near = lax.axis_index("wide") // 8, lax.axis_index("narrow")
    for a in range(8):
        square[a * 8 : a * 8 + 8, :] = tiles_ref[worker_narrow(a, high)]
    start = pl.multiple_of(worker_narrow(near, near) * 8, 8)
    square[64:72, :] = rows_ref[pl.ds(start, 8), :]
    square[72:128, :] = jnp.zeros((56, 128), jnp.float32)
    turned = square[...].T
    cols_out[...] = turned[32:36, :64]
    lane = lane_iota()
    upper = jnp.where(sub_iota() >= 4, 1, 0)
    rows = jnp.zeros((8, 128), jnp.float32)
    for g in range(4):
        part = jnp.take_along_axis(turned[8 * g : 8 * g + 8, :], 64 + (lane & 7), axis=1)
        rows = jnp.where((lane >> 3) == 2 * g + upper, part, rows)
    rows_out[...] = (rows + pltpu.roll(rows, 4, 0))[:4, :64]


def f32(*shape):
    return jax.ShapeDtypeStruct(shape, jnp.float32)


def whole(count):
    return [pl.BlockSpec(memory_space=pltpu.VMEM)] * count


def params():
    return pltpu.CompilerParams(vmem_limit_bytes=32 * 1024 * 1024)


def call(kernel, outs, *args, scratch=()):
    return pl.pallas_call(
        kernel,
        out_shape=outs,
        in_specs=whole(len(args)),
        out_specs=tuple(whole(len(outs))) if isinstance(outs, tuple) else whole(1)[0],
        scratch_shapes=scratch,
        compiler_params=params(),
    )(*args)


def exchange(x, axis, groups=None):
    return lax.all_to_all(x, axis, split_axis=0, concat_axis=0, tiled=True, axis_index_groups=groups)


def shards(images, block_slot, pairs):
    vmem = lambda *shape: pltpu.VMEM(shape, jnp.float32)
    packed = call(
        pack_kernel,
        f32(8, ROWS, 128),
        images.transpose(1, 0, 2),
        block_slot.reshape(8, 128),
        pairs[0].T,
        scratch=[vmem(4 * CH, 8, 128), pltpu.VMEM((8, 128), jnp.int32)],
    )
    near = exchange(packed, "narrow")
    relayed = call(relay_kernel, f32(ROWS, 128), packed, near)
    first = lax.ppermute(relayed, BOTH, row_routes(0))
    second = lax.ppermute(relayed, BOTH, row_routes(1))
    xc, vc = call(col_kernel, (f32(16, 4 * CH, 8, 128), f32(16, 4 * LAYERS, 8, 128)), near)
    spread = call(spread_kernel, f32(4, 2, ROWS, 128), first, second)
    far = exchange(spread, "wide", low_groups())
    own = call(
        own_kernel,
        f32(16, 128),
        first,
        second,
        xc,
        vc,
        scratch=[
            vmem(4, 4 * CH, 8, 128),
            vmem(4, 4 * LAYERS, 8, 128),
            pltpu.SMEM((2, 8, 128), jnp.float32),
            pltpu.SemaphoreType.DMA((2,)),
        ],
    )
    tiles = call(
        tile_kernel,
        f32(8, 8, 128),
        far,
        own,
        xc,
        vc,
        scratch=[
            vmem(12, 4 * CH, 8, 128),
            vmem(12, 4 * LAYERS, 8, 128),
            vmem(8, 8, 128),
            pltpu.SMEM((4, 2, 8, 128), jnp.float32),
            pltpu.SemaphoreType.DMA,
        ],
    )
    tiles = exchange(tiles, "narrow")
    rows = exchange(tiles.reshape(64, 128), BOTH, home_groups())
    rows, cols = call(place_kernel, (f32(4, 64), f32(4, 64)), tiles, rows, scratch=[vmem(128, 128)])
    return rows.T[None], cols.T[None]


def solution(mesh):
    spec = P(BOTH, None, None)
    return jax.shard_map(
        shards, mesh=mesh, in_specs=(spec, P(), spec), out_specs=(spec, spec), check_vma=False
    )
```
